128 devices in a mesh: row: 8 (over z, x_hi), col: 16 (over x_lo, y, core).
Axes of the slice: x: 4 (x_hi: 2, x_lo: 2; x = x_hi * 2 + x_lo), y: 4, z: 4, core: 2. Of those that a mesh axis runs over, the one named last changes fastest.
Arguments:
- pair: bfloat16 [1024, 1024, 128], P('row', 'col'), may hold values from -6 to 6
- left_gate: bfloat16 [128, 128], replicated, may hold values from -0.5 to 0.5
- left_proj: bfloat16 [128, 128], replicated, may hold values from -0.5 to 0.5
- right_gate: bfloat16 [128, 128], replicated, may hold values from -0.5 to 0.5
- right_proj: bfloat16 [128, 128], replicated, may hold values from -0.5 to 0.5
- out_gate: bfloat16 [128, 128], replicated, may hold values from -0.5 to 0.5
- out_proj: bfloat16 [128, 128], replicated, may hold values from -0.5 to 0.5
Outputs:
- update: bfloat16 [1024, 1024, 128], P('row', 'col')
The draws below stay inside these ranges and needn't reach their ends.
All inputs are finite; a program needn't handle non-finite values.
Results may differ from the reference program's by a relative error of at most 0.0078.
Values may be sent and summed in bfloat16 or wider, within the bound.
No kernel may reach another device: no remote copies, remote signals or barrier semaphores. Data moves between devices by JAX's collectives and lax.ppermute only.
A program may use at most 192 MiB of HBM per device.

```python
import jax
import jax.numpy as jnp
from jax import lax

C = 128
HID = 128
RES = 1024


def steps_of(rng, extent, shards, least, top_value):
    loudness = 1.0
    for axis_at, shards_of in shards:
        heights = jax.random.uniform(jax.random.fold_in(jax.random.fold_in(rng, 6), axis_at), (shards_of,), jnp.float32, least / len(shards), top_value / len(shards))
        loudness = loudness * jnp.repeat(jnp.exp(heights), extent[axis_at] // shards_of).reshape((-1,) + (1,) * (len(extent) - 1 - axis_at))
    return loudness


def scatter_about(stream_key, extent, width, most, pieces=(), kind=jnp.bfloat16):
    entries = jax.random.normal(stream_key, extent, jnp.float32) * width
    if len(pieces) > 0:
        entries = steps_of(stream_key, extent, pieces, -0.22, 0.18) * entries
    return jnp.clip(entries, min=-most, max=most).astype(kind)


def setup_inputs(seed: int = 0) -> dict:
    key_of = jax.random.split(jax.random.key(seed), 8)
    pair = scatter_about(key_of[0], (RES, RES, C), 1.0, 6.0, ((0, 8), (1, 16)))
    left_gate = scatter_about(key_of[1], (C, HID), C ** -0.5, 0.5)
    left_proj = scatter_about(key_of[2], (C, HID), C ** -0.5, 0.5)
    right_gate = scatter_about(key_of[3], (C, HID), C ** -0.5, 0.5)
    right_proj = scatter_about(key_of[4], (C, HID), C ** -0.5, 0.5)
    out_gate = scatter_about(key_of[5], (C, C), C ** -0.5, 0.5)
    out_proj = scatter_about(key_of[6], (HID, C), HID ** -0.5, 0.5)
    return dict(pair=pair, left_gate=left_gate, left_proj=left_proj, right_gate=right_gate, right_proj=right_proj, out_gate=out_gate, out_proj=out_proj)


def layer_norm(values):
    values = values.astype(jnp.float32)
    center = values - lax.optimization_barrier(jnp.mean(values, axis=-1, keepdims=True))
    spread = lax.optimization_barrier(jnp.mean(center * center, axis=-1, keepdims=True))
    return center * jax.lax.rsqrt(spread + 1e-05)

def project(normed, weight):
    flat = normed.reshape(-1, normed.shape[-1])
    out = jnp.dot(flat, weight, preferred_element_type=jnp.float32)
    return out.reshape(normed.shape[:-1] + (weight.shape[1],))

def reference(pair, left_gate, left_proj, right_gate, right_proj, out_gate, out_proj):
    normed = layer_norm(pair).astype(jnp.bfloat16)
    left = (jax.nn.sigmoid(project(normed, left_gate)) * project(normed, left_proj)).astype(jnp.bfloat16)
    right = (jax.nn.sigmoid(project(normed, right_gate)) * project(normed, right_proj)).astype(jnp.bfloat16)
    mixed = jnp.einsum('ikc,jkc->ijc', left.astype(jnp.float32), right.astype(jnp.float32))
    mixed_norm = layer_norm(mixed).astype(jnp.bfloat16)
    gated = jax.nn.sigmoid(project(normed, out_gate)) * project(mixed_norm, out_proj)
    return gated.astype(jnp.bfloat16)
```

```python
import jax
import jax.numpy as jnp
from jax import lax
from jax.experimental import pallas as pl
from jax.experimental.pallas import tpu as pltpu
from jax.sharding import PartitionSpec as P

C = 128
F32 = jnp.float32
BF16 = jnp.bfloat16
VMEM = 60 * 1024 * 1024

NT = (((1,), (1,)), ((), ()))
TN = (((0,), (0,)), ((), ()))


def sigmoid(x):
    return 0.5 * jnp.tanh(0.5 * x) + 0.5


def norm_rows(x):
    x = x.astype(F32)
    center = x - jnp.mean(x, axis=-1, keepdims=True)
    spread = jnp.mean(center * center, axis=-1, keepdims=True)
    return (center * lax.rsqrt(spread + 1e-05)).astype(BF16)


def edges_kernel(x_ref, lg_ref, lp_ref, rg_ref, rp_ref, o_ref, w_ref, stage):
    @pl.when(pl.program_id(0) == 0)
    def _():
        for n, ref in enumerate((lg_ref, lp_ref, rg_ref, rp_ref)):
            w_ref[n * C : (n + 1) * C, :] = ref[...].T

    steps = x_ref.shape[1]
    for s in range(0, steps, 2):
        x = jnp.concatenate(
            [x_ref[0, s], x_ref[1, s], x_ref[0, s + 1], x_ref[1, s + 1]], axis=0
        )
        p = lax.dot_general(w_ref[...], norm_rows(x), NT, preferred_element_type=F32)
        for side in range(2):
            at = 2 * C * side
            edge = sigmoid(p[at : at + C]) * p[at + C : at + 2 * C]
            stage[:, side, s, :] = edge[:, :C]
            stage[:, side, s + 1, :] = edge[:, C:]
    o_ref[...] = stage[...].astype(BF16)


def edges(pair4, lg, lp, rg, rp):
    _, steps, cols, ch = pair4.shape
    block = 16
    whole = pl.BlockSpec((C, C), lambda n: (0, 0))
    return pl.pallas_call(
        edges_kernel,
        grid=(steps // block,),
        in_specs=[pl.BlockSpec((2, block, cols, ch), lambda n: (0, n, 0, 0))] + [whole] * 4,
        out_specs=pl.BlockSpec((C, 2, block, 2 * cols), lambda n: (0, 0, n, 0)),
        out_shape=jax.ShapeDtypeStruct((C, 2, steps, 2 * cols), BF16),
        scratch_shapes=[
            pltpu.VMEM((4 * C, C), BF16),
            pltpu.VMEM((C, 2, block, 2 * cols), F32),
        ],
        compiler_params=pltpu.CompilerParams(vmem_limit_bytes=VMEM),
        cost_estimate=pl.CostEstimate(
            flops=2 * 4 * C * C * 8192, bytes_accessed=6 << 20, transcendentals=2 << 20
        ),
        name="edges",
    )(pair4, lg, lp, rg, rp)


def gate_kernel(x_ref, w_ref, o_ref):
    n = x_ref.shape[0]
    rows = x_ref.shape[1]
    for i in range(0, n, 4):
        x = x_ref[i : i + 4].reshape(4 * rows, C)
        p = jnp.dot(norm_rows(x), w_ref[...], preferred_element_type=F32)
        o_ref[i : i + 4] = sigmoid(p).reshape(4, rows, C)


def out_gates(pair, w):
    rows, cols, ch = pair.shape
    block = 16
    return pl.pallas_call(
        gate_kernel,
        grid=(rows // block,),
        in_specs=[
            pl.BlockSpec((block, cols, ch), lambda n: (n, 0, 0)),
            pl.BlockSpec((C, C), lambda n: (0, 0)),
        ],
        out_specs=pl.BlockSpec((block, cols, ch), lambda n: (n, 0, 0)),
        out_shape=jax.ShapeDtypeStruct((rows, cols, ch), F32),
        compiler_params=pltpu.CompilerParams(vmem_limit_bytes=VMEM),
        cost_estimate=pl.CostEstimate(
            flops=2 * C * C * 8192, bytes_accessed=6 << 20, transcendentals=1 << 20
        ),
        name="out_gates",
    )(pair, w)


def turn(top, low):
    h = top.shape[1] // 2
    return (
        jnp.concatenate([top[:, :h], low[:, :h]], axis=1),
        jnp.concatenate([top[:, h:], low[:, h:]], axis=1),
    )


def mix_kernel(l_ref, r_ref, o_ref, left, right):
    def gather(src, dst):
        rows, cols = src.shape[0], src.shape[1]
        s = src.shape[3]
        for r in range(rows):
            for q in range(0, cols, 2):
                a, b = turn(src[r, q, 0], src[r, q + 1, 0])
                dst[2 * r * s : 2 * r * s + s, q * s : q * s + 2 * s] = a
                dst[2 * r * s + s : 2 * r * s + 2 * s, q * s : q * s + 2 * s] = b

    @pl.when(pl.program_id(0) == 0)
    def _():
        gather(l_ref, left)

    gather(r_ref, right)
    s = o_ref.shape[2]
    for r in range(o_ref.shape[0]):
        m = lax.dot_general(
            left[2 * r * s : 2 * r * s + 2 * s, :], right[...], NT, preferred_element_type=F32
        ).astype(BF16)
        for q in range(0, o_ref.shape[1], 2):
            a, b = turn(m[:s, q * s : q * s + 2 * s], m[s:, q * s : q * s + 2 * s])
            o_ref[r, q] = a
            o_ref[r, q + 1] = b


def mix(got, rows, cols):
    steps, lanes = got.shape[2], got.shape[3]
    got = got.reshape(rows, cols, 2, steps, lanes)
    blocks = 4
    return pl.pallas_call(
        mix_kernel,
        grid=(blocks,),
        in_specs=[
            pl.BlockSpec((rows, cols, 1, steps, lanes), lambda n: (0, 0, 0, 0, 0)),
            pl.BlockSpec((rows // blocks, cols, 1, steps, lanes), lambda n: (n, 0, 1, 0, 0)),
        ],
        out_specs=pl.BlockSpec((rows, cols // blocks, steps, lanes), lambda n: (0, n, 0, 0)),
        out_shape=jax.ShapeDtypeStruct((rows, cols, steps, lanes), BF16),
        scratch_shapes=[
            pltpu.VMEM((2 * rows * steps, cols * steps), BF16),
            pltpu.VMEM((2 * rows * steps // blocks, cols * steps), BF16),
        ],
        compiler_params=pltpu.CompilerParams(vmem_limit_bytes=VMEM),
        cost_estimate=pl.CostEstimate(
            flops=2 << 30, bytes_accessed=6 << 20, transcendentals=0
        ),
        name="mix",
    )(got, got).reshape(rows * cols, steps, lanes)


def update_kernel(m_ref, g_ref, w_ref, o_ref, stage):
    m = m_ref[...].astype(F32)
    center = m - jnp.mean(m, axis=0, keepdims=True)
    spread = jnp.mean(center * center, axis=0, keepdims=True)
    stage[...] = center * lax.rsqrt(spread + 1e-05)
    cols = o_ref.shape[2]
    for s in range(m_ref.shape[1]):
        x = stage[:, s, :].astype(BF16)
        p = lax.dot_general(x, w_ref[...], TN, preferred_element_type=F32)
        o_ref[0, s] = (p[:cols] * g_ref[0, s]).astype(BF16)
        o_ref[1, s] = (p[cols:] * g_ref[1, s]).astype(BF16)


def update(mixed, gate4, w):
    _, steps, cols, ch = gate4.shape
    block = 16
    spec = pl.BlockSpec((2, block, cols, ch), lambda n: (0, n, 0, 0))
    return pl.pallas_call(
        update_kernel,
        grid=(steps // block,),
        in_specs=[
            pl.BlockSpec((C, block, 2 * cols), lambda n: (0, n, 0)),
            spec,
            pl.BlockSpec((C, C), lambda n: (0, 0)),
        ],
        out_specs=spec,
        out_shape=jax.ShapeDtypeStruct((2, steps, cols, ch), BF16),
        scratch_shapes=[pltpu.VMEM((C, block, 2 * cols), F32)],
        compiler_params=pltpu.CompilerParams(vmem_limit_bytes=VMEM),
        cost_estimate=pl.CostEstimate(
            flops=2 * C * C * 8192, bytes_accessed=8 << 20, transcendentals=0
        ),
        name="update",
    )(mixed, gate4, w)


def on_device(rows, cols, pair, left_gate, left_proj, right_gate, right_proj, out_gate, out_proj):
    ni, nj, ch = pair.shape
    pair4 = pair.reshape(2, ni // 2, nj, ch)
    sent = edges(pair4, left_gate, left_proj, right_gate, right_proj)
    got = lax.all_to_all(sent, ("row", "col"), 0, 0, tiled=True)
    gate = out_gates(pair, out_gate)
    mixed = mix(got, rows, cols)
    mixed = lax.all_to_all(mixed, ("row", "col"), 0, 0, tiled=True)
    out = update(mixed, gate.reshape(2, ni // 2, nj, ch), out_proj)
    return out.reshape(ni, nj, ch)


def solution(mesh):
    rows, cols = mesh.shape["row"], mesh.shape["col"]

    def body(*args):
        return on_device(rows, cols, *args)

    return jax.shard_map(
        body,
        mesh=mesh,
        in_specs=(P("row", "col", None), P(), P(), P(), P(), P(), P()),
        out_specs=P("row", "col", None),
        check_vma=False,
    )
```

```python
import jax
import jax.numpy as jnp
from jax import lax
from jax.experimental import pallas as pl
from jax.experimental.pallas import tpu as pltpu
from jax.sharding import PartitionSpec as P

C = 128
F32 = jnp.float32
BF16 = jnp.bfloat16
BLOCK = 16
PITCH = BLOCK + 1
VMEM = 24 * 1024 * 1024
FULL = 63 * 1024 * 1024

NT = (((1,), (1,)), ((), ()))
TN = (((0,), (0,)), ((), ()))


def sigmoid(x):
    return 0.5 * jnp.tanh(0.5 * x) + 0.5


def norm_rows(x):
    x = x.astype(F32)
    center = x - jnp.mean(x, axis=-1, keepdims=True)
    spread = jnp.mean(center * center, axis=-1, keepdims=True)
    return (center * lax.rsqrt(spread + 1e-05)).astype(BF16)


def edges_kernel(
    x_hbm, lg_hbm, lp_hbm, rg_hbm, rp_hbm, o_hbm,
    x_ref, o_ref, w_in, w_ref, stage_l, stage_r, x_sem, o_sem, w_sem
):
    weights = [
        pltpu.make_async_copy(ref, w_in.at[n], w_sem.at[n])
        for n, ref in enumerate((lg_hbm, lp_hbm, rg_hbm, rp_hbm))
    ]
    parts = x_sem.shape[0]
    part = x_ref.shape[1] // parts
    loads = [
        pltpu.make_async_copy(
            x_hbm.at[:, pl.ds(n * part, part)], x_ref.at[:, pl.ds(n * part, part)], x_sem.at[n]
        )
        for n in range(parts)
    ]
    for copy in weights + loads:
        copy.start()
    for n, copy in enumerate(weights):
        copy.wait()
        w_ref[n * C : (n + 1) * C, :] = w_in[n].T * 0.5

    stores = []
    for n, copy in enumerate(loads):
        copy.wait()
        first = n * part
        for s in range(0, part, 2):
            x = jnp.concatenate(
                [x_ref[0, first + s], x_ref[1, first + s]]
                + [x_ref[0, first + s + 1], x_ref[1, first + s + 1]],
                axis=0,
            )
            p = lax.dot_general(w_ref[...], norm_rows(x), NT, preferred_element_type=F32)
            for side, stage in enumerate((stage_l, stage_r)):
                at = 2 * C * side
                half = p[at + C : at + 2 * C]
                edge = jnp.tanh(p[at : at + C]) * half + half
                stage[pl.ds(s, C, stride=PITCH), :] = edge[:, :C]
                stage[pl.ds(s + 1, C, stride=PITCH), :] = edge[:, C:]
        for side, stage in enumerate((stage_l, stage_r)):
            for c in range(C):
                o_ref[c, side, first : first + part, :] = stage[
                    c * PITCH : c * PITCH + part, :
                ].astype(BF16)
        store = pltpu.make_async_copy(
            o_ref.at[:, :, pl.ds(first, part)], o_hbm.at[:, :, pl.ds(first, part)], o_sem.at[n]
        )
        store.start()
        stores.append(store)
    for store in stores:
        store.wait()


def edges(pair4, lg, lp, rg, rp):
    _, steps, cols, ch = pair4.shape
    parts = steps // BLOCK
    hbm = pl.BlockSpec(memory_space=pltpu.HBM)
    stage = pltpu.VMEM((C * PITCH, 2 * cols), F32)
    return pl.pallas_call(
        edges_kernel,
        in_specs=[hbm] * 5,
        out_specs=hbm,
        out_shape=jax.ShapeDtypeStruct((C, 2, steps, 2 * cols), BF16),
        scratch_shapes=[
            pltpu.VMEM(pair4.shape, BF16),
            pltpu.VMEM((C, 2, steps, 2 * cols), BF16),
            pltpu.VMEM((4, C, C), BF16),
            pltpu.VMEM((4 * C, C), BF16),
            stage,
            stage,
            pltpu.SemaphoreType.DMA((parts,)),
            pltpu.SemaphoreType.DMA((parts,)),
            pltpu.SemaphoreType.DMA((4,)),
        ],
        compiler_params=pltpu.CompilerParams(vmem_limit_bytes=FULL),
        cost_estimate=pl.CostEstimate(
            flops=2 * 4 * C * C * 8192, bytes_accessed=6 << 20, transcendentals=2 << 20
        ),
        name="edges",
    )(pair4, lg, lp, rg, rp)


def gate_kernel(x_ref, w_ref, o_ref):
    n = x_ref.shape[0]
    rows = x_ref.shape[1]
    for i in range(0, n, 4):
        x = x_ref[i : i + 4].reshape(4 * rows, C)
        p = jnp.dot(norm_rows(x), w_ref[...], preferred_element_type=F32)
        o_ref[i : i + 4] = sigmoid(p).reshape(4, rows, C)


def out_gates(pair, w):
    rows, cols, ch = pair.shape
    block = 16
    return pl.pallas_call(
        gate_kernel,
        grid=(rows // block,),
        in_specs=[
            pl.BlockSpec((block, cols, ch), lambda n: (n, 0, 0)),
            pl.BlockSpec((C, C), lambda n: (0, 0)),
        ],
        out_specs=pl.BlockSpec((block, cols, ch), lambda n: (n, 0, 0)),
        out_shape=jax.ShapeDtypeStruct((rows, cols, ch), F32),
        compiler_params=pltpu.CompilerParams(vmem_limit_bytes=FULL),
        cost_estimate=pl.CostEstimate(
            flops=2 * C * C * 8192, bytes_accessed=6 << 20, transcendentals=1 << 20
        ),
        name="out_gates",
    )(pair, w)


def turn(top, low):
    h = top.shape[1] // 2
    return (
        jnp.concatenate([top[:, :h], low[:, :h]], axis=1),
        jnp.concatenate([top[:, h:], low[:, h:]], axis=1),
    )


def mix_kernel(got_ref, o_ref, left, right):
    rows, cols, _, s, _ = got_ref.shape
    for side, dst in enumerate((left, right)):
        for r in range(rows):
            for q in range(0, cols, 2):
                a, b = turn(got_ref[r, q, side], got_ref[r, q + 1, side])
                dst[2 * r * s : 2 * r * s + s, q * s : q * s + 2 * s] = a
                dst[2 * r * s + s : 2 * r * s + 2 * s, q * s : q * s + 2 * s] = b
    wide = 4
    for n in range(0, cols, wide):
        m = lax.dot_general(
            left[...], right[n * s : (n + wide) * s, :], NT, preferred_element_type=F32
        ).astype(BF16)
        for r in range(rows):
            top = m[2 * r * s : 2 * r * s + s]
            low = m[2 * r * s + s : 2 * r * s + 2 * s]
            for q in range(0, wide, 2):
                at = slice(q * s, q * s + 2 * s)
                a, b = turn(top[:, at], low[:, at])
                o_ref[r, n + q] = a
                o_ref[r, n + q + 1] = b


def mix(got, rows, cols):
    steps, lanes = got.shape[2], got.shape[3]
    got = got.reshape(rows, cols, 2, steps, lanes)
    edge = pltpu.VMEM((2 * rows * steps, cols * steps), BF16)
    return pl.pallas_call(
        mix_kernel,
        in_specs=[pl.BlockSpec(memory_space=pltpu.VMEM)],
        out_specs=pl.BlockSpec(memory_space=pltpu.VMEM),
        out_shape=jax.ShapeDtypeStruct((rows, cols, steps, lanes), BF16),
        scratch_shapes=[edge, edge],
        compiler_params=pltpu.CompilerParams(vmem_limit_bytes=VMEM),
        cost_estimate=pl.CostEstimate(
            flops=2 << 30, bytes_accessed=6 << 20, transcendentals=0
        ),
        name="mix",
    )(got).reshape(rows * cols, steps, lanes)


def tree_sum(term):
    sums = [term(c) for c in range(4)]
    for c in range(4, C):
        sums[c % 4] += term(c)
    return (sums[0] + sums[1]) + (sums[2] + sums[3])


def update_kernel(
    m_hbm, g_hbm, w_hbm, o_hbm, m_ref, g_ref, w_ref, stage, o_ref, m_sem, g_sem, w_sem, o_sem
):
    parts = o_sem.shape[0]
    part = o_ref.shape[1] // parts
    cols = o_ref.shape[2]
    w_load = pltpu.make_async_copy(w_hbm, w_ref, w_sem)
    w_load.start()
    loads = []
    for n in range(parts):
        at = pl.ds(n * part, part)
        m_load = pltpu.make_async_copy(m_hbm.at[:, at], m_ref.at[:, at], m_sem.at[n])
        g_load = pltpu.make_async_copy(g_hbm.at[:, at], g_ref.at[:, at], g_sem.at[n])
        m_load.start()
        g_load.start()
        loads.append((m_load, g_load))
    w_load.wait()
    stores = []
    for n in range(parts):
        first = n * part

        for load in loads[n]:
            load.wait()
        def channel(c):
            return m_ref[c, first : first + part, :].astype(F32)

        mean = tree_sum(channel) * (1 / C)
        spread = tree_sum(lambda c: jnp.square(channel(c) - mean)) * (1 / C)
        scale = lax.rsqrt(spread + 1e-05)
        for c in range(C):
            stage[c * PITCH : c * PITCH + part, :] = (channel(c) - mean) * scale
        for s in range(part):
            x = stage[pl.ds(s, C, stride=PITCH), :].astype(BF16)
            p = lax.dot_general(x, w_ref[...], TN, preferred_element_type=F32)
            o_ref[0, first + s] = (p[:cols] * g_ref[0, first + s]).astype(BF16)
            o_ref[1, first + s] = (p[cols:] * g_ref[1, first + s]).astype(BF16)
        at = pl.ds(first, part)
        store = pltpu.make_async_copy(o_ref.at[:, at], o_hbm.at[:, at], o_sem.at[n])
        store.start()
        stores.append(store)
    for store in stores:
        store.wait()


def update(mixed, gate4, w):
    _, steps, cols, ch = gate4.shape
    parts = steps // BLOCK
    hbm = pl.BlockSpec(memory_space=pltpu.HBM)
    sems = pltpu.SemaphoreType.DMA((parts,))
    return pl.pallas_call(
        update_kernel,
        in_specs=[hbm] * 3,
        out_specs=hbm,
        out_shape=jax.ShapeDtypeStruct(gate4.shape, BF16),
        scratch_shapes=[
            pltpu.VMEM(mixed.shape, BF16),
            pltpu.VMEM(gate4.shape, F32),
            pltpu.VMEM((C, C), BF16),
            pltpu.VMEM((C * PITCH, 2 * cols), F32),
            pltpu.VMEM(gate4.shape, BF16),
            sems,
            sems,
            pltpu.SemaphoreType.DMA,
            sems,
        ],
        compiler_params=pltpu.CompilerParams(vmem_limit_bytes=FULL),
        cost_estimate=pl.CostEstimate(
            flops=2 * C * C * 8192, bytes_accessed=8 << 20, transcendentals=0
        ),
        name="update",
    )(mixed, gate4, w)


def on_device(rows, cols, pair, left_gate, left_proj, right_gate, right_proj, out_gate, out_proj):
    ni, nj, ch = pair.shape
    pair4 = pair.reshape(2, ni // 2, nj, ch)
    sent = edges(pair4, left_gate, left_proj, right_gate, right_proj)
    got = lax.all_to_all(sent, ("row", "col"), 0, 0, tiled=True)
    gate = out_gates(pair, out_gate)
    mixed = mix(got, rows, cols)
    mixed = lax.all_to_all(mixed, ("row", "col"), 0, 0, tiled=True)
    out = update(mixed, gate.reshape(2, ni // 2, nj, ch), out_proj)
    return out.reshape(ni, nj, ch)


def solution(mesh):
    rows, cols = mesh.shape["row"], mesh.shape["col"]

    def body(*args):
        return on_device(rows, cols, *args)

    return jax.shard_map(
        body,
        mesh=mesh,
        in_specs=(P("row", "col", None), P(), P(), P(), P(), P(), P()),
        out_specs=P("row", "col", None),
        check_vma=False,
    )
```

```python
import jax
import jax.numpy as jnp
from jax import lax
from jax.experimental import pallas as pl
from jax.experimental.pallas import tpu as pltpu
from jax.sharding import PartitionSpec as P

C = 128
F32 = jnp.float32
BF16 = jnp.bfloat16
BLOCK = 16
PITCH = BLOCK + 1
VMEM = 24 * 1024 * 1024
FULL = 63 * 1024 * 1024

NT = (((1,), (1,)), ((), ()))
TN = (((0,), (0,)), ((), ()))


def norm_rows(x):
    x = x.astype(F32)
    center = x - jnp.mean(x, axis=-1, keepdims=True)
    spread = jnp.mean(center * center, axis=-1, keepdims=True)
    return (center * lax.rsqrt(spread + 1e-05)).astype(BF16)


def edges_kernel(
    x_hbm, lg_hbm, lp_hbm, rg_hbm, rp_hbm, og_hbm, o_hbm, g_hbm,
    x_ref, o_ref, g_ref, w_in, w_ref, stage_l, stage_r, x_sem, o_sem, g_sem, w_sem
):
    weights = [
        pltpu.make_async_copy(ref, w_in.at[n], w_sem.at[n])
        for n, ref in enumerate((lg_hbm, lp_hbm, rg_hbm, rp_hbm, og_hbm))
    ]
    parts = x_sem.shape[0]
    part = x_ref.shape[1] // parts
    loads = [
        pltpu.make_async_copy(
            x_hbm.at[:, pl.ds(n * part, part)], x_ref.at[:, pl.ds(n * part, part)], x_sem.at[n]
        )
        for n in range(parts)
    ]
    for copy in weights + loads:
        copy.start()
    for n, copy in enumerate(weights):
        copy.wait()
        if n < 4:
            w_ref[n * C : (n + 1) * C, :] = w_in[n].T * 0.5
        else:
            w_in[n] = w_in[n] * 0.5

    stores = []
    for n, copy in enumerate(loads):
        copy.wait()
        first = n * part
        for s in range(0, part, 2):
            x = jnp.concatenate(
                [x_ref[0, first + s], x_ref[1, first + s]]
                + [x_ref[0, first + s + 1], x_ref[1, first + s + 1]],
                axis=0,
            )
            x = norm_rows(x)
            q = jnp.dot(x, w_in[4], preferred_element_type=F32)
            q = (jnp.tanh(q) * 0.5 + 0.5).astype(BF16).reshape(2, 2, -1, C)
            g_ref[0, first + s], g_ref[1, first + s] = q[0, 0], q[0, 1]
            g_ref[0, first + s + 1], g_ref[1, first + s + 1] = q[1, 0], q[1, 1]
            p = lax.dot_general(w_ref[...], x, NT, preferred_element_type=F32)
            for side, stage in enumerate((stage_l, stage_r)):
                at = 2 * C * side
                half = p[at + C : at + 2 * C]
                edge = jnp.tanh(p[at : at + C]) * half + half
                stage[pl.ds(s, C, stride=PITCH), :] = edge[:, :C]
                stage[pl.ds(s + 1, C, stride=PITCH), :] = edge[:, C:]
        for side, stage in enumerate((stage_l, stage_r)):
            for c in range(C):
                o_ref[c, side, first : first + part, :] = stage[
                    c * PITCH : c * PITCH + part, :
                ].astype(BF16)
        at = pl.ds(first, part)
        for store in (
            pltpu.make_async_copy(o_ref.at[:, :, at], o_hbm.at[:, :, at], o_sem.at[n]),
            pltpu.make_async_copy(g_ref.at[:, at], g_hbm.at[:, at], g_sem.at[n]),
        ):
            store.start()
            stores.append(store)
    for store in stores:
        store.wait()


def edges(pair4, lg, lp, rg, rp, og):
    _, steps, cols, ch = pair4.shape
    parts = steps // BLOCK
    hbm = pl.BlockSpec(memory_space=pltpu.HBM)
    stage = pltpu.VMEM((C * PITCH, 2 * cols), F32)
    return pl.pallas_call(
        edges_kernel,
        in_specs=[hbm] * 6,
        out_specs=[hbm, hbm],
        out_shape=[
            jax.ShapeDtypeStruct((C, 2, steps, 2 * cols), BF16),
            jax.ShapeDtypeStruct(pair4.shape, BF16),
        ],
        scratch_shapes=[
            pltpu.VMEM(pair4.shape, BF16),
            pltpu.VMEM((C, 2, steps, 2 * cols), BF16),
            pltpu.VMEM(pair4.shape, BF16),
            pltpu.VMEM((5, C, C), BF16),
            pltpu.VMEM((4 * C, C), BF16),
            stage,
            stage,
            pltpu.SemaphoreType.DMA((parts,)),
            pltpu.SemaphoreType.DMA((parts,)),
            pltpu.SemaphoreType.DMA((parts,)),
            pltpu.SemaphoreType.DMA((5,)),
        ],
        compiler_params=pltpu.CompilerParams(vmem_limit_bytes=FULL),
        cost_estimate=pl.CostEstimate(
            flops=2 * 5 * C * C * 8192, bytes_accessed=8 << 20, transcendentals=2 << 20
        ),
        name="edges",
    )(pair4, lg, lp, rg, rp, og)


def turn(top, low):
    h = top.shape[1] // 2
    return (
        jnp.concatenate([top[:, :h], low[:, :h]], axis=1),
        jnp.concatenate([top[:, h:], low[:, h:]], axis=1),
    )


def mix_kernel(got_ref, o_ref, left, right):
    rows, cols, _, s, _ = got_ref.shape
    for side, dst in enumerate((left, right)):
        for r in range(rows):
            for q in range(0, cols, 2):
                a, b = turn(got_ref[r, q, side], got_ref[r, q + 1, side])
                dst[2 * r * s : 2 * r * s + s, q * s : q * s + 2 * s] = a
                dst[2 * r * s + s : 2 * r * s + 2 * s, q * s : q * s + 2 * s] = b
    wide = 4
    for n in range(0, cols, wide):
        m = lax.dot_general(
            left[...], right[n * s : (n + wide) * s, :], NT, preferred_element_type=F32
        ).astype(BF16)
        for r in range(rows):
            top = m[2 * r * s : 2 * r * s + s]
            low = m[2 * r * s + s : 2 * r * s + 2 * s]
            for q in range(0, wide, 2):
                at = slice(q * s, q * s + 2 * s)
                a, b = turn(top[:, at], low[:, at])
                o_ref[r, n + q] = a
                o_ref[r, n + q + 1] = b


def mix(got, rows, cols):
    steps, lanes = got.shape[2], got.shape[3]
    got = got.reshape(rows, cols, 2, steps, lanes)
    edge = pltpu.VMEM((2 * rows * steps, cols * steps), BF16)
    return pl.pallas_call(
        mix_kernel,
        in_specs=[pl.BlockSpec(memory_space=pltpu.VMEM)],
        out_specs=pl.BlockSpec(memory_space=pltpu.VMEM),
        out_shape=jax.ShapeDtypeStruct((rows, cols, steps, lanes), BF16),
        scratch_shapes=[edge, edge],
        compiler_params=pltpu.CompilerParams(vmem_limit_bytes=VMEM),
        cost_estimate=pl.CostEstimate(
            flops=2 << 30, bytes_accessed=6 << 20, transcendentals=0
        ),
        name="mix",
    )(got).reshape(rows * cols, steps, lanes)


def tree_sum(term):
    sums = [term(c) for c in range(4)]
    for c in range(4, C):
        sums[c % 4] += term(c)
    return (sums[0] + sums[1]) + (sums[2] + sums[3])


def update_kernel(
    m_ref, g_ref, w_ref, o_hbm, stage, o_ref, o_sem
):
    parts = o_sem.shape[0]
    part = o_ref.shape[1] // parts
    cols = o_ref.shape[2]
    stores = []
    for n in range(parts):
        first = n * part

        def channel(c):
            return m_ref[c, first : first + part, :].astype(F32)

        mean = tree_sum(channel) * (1 / C)
        spread = tree_sum(lambda c: jnp.square(channel(c) - mean)) * (1 / C)
        scale = lax.rsqrt(spread + 1e-05)
        for c in range(C):
            stage[c * PITCH : c * PITCH + part, :] = (channel(c) - mean) * scale
        for s in range(part):
            x = stage[pl.ds(s, C, stride=PITCH), :].astype(BF16)
            p = lax.dot_general(x, w_ref[...], TN, preferred_element_type=F32)
            o_ref[0, first + s] = (p[:cols] * g_ref[0, first + s]).astype(BF16)
            o_ref[1, first + s] = (p[cols:] * g_ref[1, first + s]).astype(BF16)
        at = pl.ds(first, part)
        store = pltpu.make_async_copy(o_ref.at[:, at], o_hbm.at[:, at], o_sem.at[n])
        store.start()
        stores.append(store)
    for store in stores:
        store.wait()


def update(mixed, gate4, w):
    _, steps, cols, ch = gate4.shape
    parts = steps // BLOCK
    hbm = pl.BlockSpec(memory_space=pltpu.HBM)
    sems = pltpu.SemaphoreType.DMA((parts,))
    return pl.pallas_call(
        update_kernel,
        in_specs=[pl.BlockSpec(memory_space=pltpu.VMEM)] * 3,
        out_specs=hbm,
        out_shape=jax.ShapeDtypeStruct(gate4.shape, BF16),
        scratch_shapes=[
            pltpu.VMEM((C * PITCH, 2 * cols), F32),
            pltpu.VMEM(gate4.shape, BF16),
            sems,
        ],
        compiler_params=pltpu.CompilerParams(vmem_limit_bytes=VMEM),
        cost_estimate=pl.CostEstimate(
            flops=2 * C * C * 8192, bytes_accessed=8 << 20, transcendentals=0
        ),
        name="update",
    )(mixed, gate4, w)


def on_device(rows, cols, pair, left_gate, left_proj, right_gate, right_proj, out_gate, out_proj):
    ni, nj, ch = pair.shape
    pair4 = pair.reshape(2, ni // 2, nj, ch)
    sent, gate = edges(pair4, left_gate, left_proj, right_gate, right_proj, out_gate)
    got = lax.all_to_all(sent, ("row", "col"), 0, 0, tiled=True)
    mixed = mix(got, rows, cols)
    mixed = lax.all_to_all(mixed, ("row", "col"), 0, 0, tiled=True)
    out = update(mixed, gate, out_proj)
    return out.reshape(ni, nj, ch)


def solution(mesh):
    rows, cols = mesh.shape["row"], mesh.shape["col"]

    def body(*args):
        return on_device(rows, cols, *args)

    return jax.shard_map(
        body,
        mesh=mesh,
        in_specs=(P("row", "col", None), P(), P(), P(), P(), P(), P()),
        out_specs=P("row", "col", None),
        check_vma=False,
    )
```

```python
import functools

import jax
import jax.numpy as jnp
import numpy as np
from jax import lax
from jax.experimental import pallas as pl
from jax.experimental.pallas import tpu as pltpu
from jax.sharding import PartitionSpec as P

C = 128
F32 = jnp.float32
BF16 = jnp.bfloat16
BLOCK = 16
PITCH = BLOCK + 1
VMEM = 24 * 1024 * 1024
FULL = 63 * 1024 * 1024

NT = (((1,), (1,)), ((), ()))
TN = (((0,), (0,)), ((), ()))


def norm_rows(x):
    x = x.astype(F32)
    center = x - jnp.mean(x, axis=-1, keepdims=True)
    spread = jnp.mean(center * center, axis=-1, keepdims=True)
    return (center * lax.rsqrt(spread + 1e-05)).astype(BF16)


def edges_kernel(
    x_hbm, lg_hbm, lp_hbm, rg_hbm, rp_hbm, og_hbm, o_hbm, g_hbm,
    x_ref, o_ref, g_ref, w_in, w_ref, stage_l, stage_r, x_sem, o_sem, g_sem, w_sem
):
    weights = [
        pltpu.make_async_copy(ref, w_in.at[n], w_sem.at[n])
        for n, ref in enumerate((lg_hbm, lp_hbm, rg_hbm, rp_hbm, og_hbm))
    ]
    parts = x_sem.shape[0]
    part = x_ref.shape[1] // parts
    loads = [
        pltpu.make_async_copy(
            x_hbm.at[:, pl.ds(n * part, part)], x_ref.at[:, pl.ds(n * part, part)], x_sem.at[n]
        )
        for n in range(parts)
    ]
    for copy in weights + loads:
        copy.start()
    for n, copy in enumerate(weights):
        copy.wait()
        if n < 4:
            w_ref[n * C : (n + 1) * C, :] = w_in[n].T * 0.5
        else:
            w_in[n] = w_in[n] * 0.5

    for copy in loads:
        copy.wait()
    stores = []
    for n in range(parts):
        first = n * part
        for s in range(0, part, 2):
            x = jnp.concatenate(
                [x_ref[0, first + s], x_ref[1, first + s]]
                + [x_ref[0, first + s + 1], x_ref[1, first + s + 1]],
                axis=0,
            )
            x = norm_rows(x)
            q = jnp.dot(x, w_in[4], preferred_element_type=F32)
            q = (jnp.tanh(q) * 0.5 + 0.5).astype(BF16).reshape(2, 2, -1, C)
            g_ref[0, first + s], g_ref[1, first + s] = q[0, 0], q[0, 1]
            g_ref[0, first + s + 1], g_ref[1, first + s + 1] = q[1, 0], q[1, 1]
            p = lax.dot_general(w_ref[...], x, NT, preferred_element_type=F32)
            for side, stage in enumerate((stage_l, stage_r)):
                at = 2 * C * side
                half = p[at + C : at + 2 * C]
                edge = jnp.tanh(p[at : at + C]) * half + half
                stage[pl.ds(s, C, stride=PITCH), :] = edge[:, :C]
                stage[pl.ds(s + 1, C, stride=PITCH), :] = edge[:, C:]
        for side, stage in enumerate((stage_l, stage_r)):
            for c in range(C):
                o_ref[c, side, first : first + part, :] = stage[
                    c * PITCH : c * PITCH + part, :
                ].astype(BF16)
        at = pl.ds(first, part)
        for store in (
            pltpu.make_async_copy(o_ref.at[:, :, at], o_hbm.at[:, :, at], o_sem.at[n]),
            pltpu.make_async_copy(g_ref.at[:, at], g_hbm.at[:, at], g_sem.at[n]),
        ):
            store.start()
            stores.append(store)
    for store in stores:
        store.wait()


def edges(pair4, lg, lp, rg, rp, og):
    _, steps, cols, ch = pair4.shape
    parts = steps // BLOCK
    hbm = pl.BlockSpec(memory_space=pltpu.HBM)
    stage = pltpu.VMEM((C * PITCH, 2 * cols), F32)
    return pl.pallas_call(
        edges_kernel,
        in_specs=[hbm] * 6,
        out_specs=[hbm, hbm],
        out_shape=[
            jax.ShapeDtypeStruct((C, 2, steps, 2 * cols), BF16),
            jax.ShapeDtypeStruct(pair4.shape, BF16),
        ],
        scratch_shapes=[
            pltpu.VMEM(pair4.shape, BF16),
            pltpu.VMEM((C, 2, steps, 2 * cols), BF16),
            pltpu.VMEM(pair4.shape, BF16),
            pltpu.VMEM((5, C, C), BF16),
            pltpu.VMEM((4 * C, C), BF16),
            stage,
            stage,
            pltpu.SemaphoreType.DMA((parts,)),
            pltpu.SemaphoreType.DMA((parts,)),
            pltpu.SemaphoreType.DMA((parts,)),
            pltpu.SemaphoreType.DMA((5,)),
        ],
        compiler_params=pltpu.CompilerParams(vmem_limit_bytes=FULL),
        cost_estimate=pl.CostEstimate(
            flops=2 * 5 * C * C * 8192, bytes_accessed=8 << 20, transcendentals=2 << 20
        ),
        name="edges",
    )(pair4, lg, lp, rg, rp, og)


def turn(top, low):
    h = top.shape[1] // 2
    return (
        jnp.concatenate([top[:, :h], low[:, :h]], axis=1),
        jnp.concatenate([top[:, h:], low[:, h:]], axis=1),
    )


def mix_kernel(source, target, got_ref, o_ref, left, right):
    rows, cols = source.shape
    s = got_ref.shape[2]
    for side, dst in enumerate((left, right)):
        for r in range(rows):
            for q in range(0, cols, 2):
                a, b = turn(got_ref[source[r, q], side], got_ref[source[r, q + 1], side])
                dst[2 * r * s : 2 * r * s + s, q * s : q * s + 2 * s] = a
                dst[2 * r * s + s : 2 * r * s + 2 * s, q * s : q * s + 2 * s] = b
    wide = 4
    for n in range(0, cols, wide):
        m = lax.dot_general(
            left[...], right[n * s : (n + wide) * s, :], NT, preferred_element_type=F32
        ).astype(BF16)
        for r in range(rows):
            top = m[2 * r * s : 2 * r * s + s]
            low = m[2 * r * s + s : 2 * r * s + 2 * s]
            for q in range(0, wide, 2):
                at = slice(q * s, q * s + 2 * s)
                a, b = turn(top[:, at], low[:, at])
                o_ref[target[r, n + q]] = a
                o_ref[target[r, n + q + 1]] = b


def mix(got, source, target):
    count, _, steps, lanes = got.shape
    rows, cols = source.shape
    edge = pltpu.VMEM((2 * rows * steps, cols * steps), BF16)
    return pl.pallas_call(
        functools.partial(mix_kernel, source, target),
        in_specs=[pl.BlockSpec(memory_space=pltpu.VMEM)],
        out_specs=pl.BlockSpec(memory_space=pltpu.VMEM),
        out_shape=jax.ShapeDtypeStruct((count, steps, lanes), BF16),
        scratch_shapes=[edge, edge],
        compiler_params=pltpu.CompilerParams(vmem_limit_bytes=VMEM),
        cost_estimate=pl.CostEstimate(
            flops=2 << 30, bytes_accessed=6 << 20, transcendentals=0
        ),
        name="mix",
    )(got)


def tree_sum(term):
    sums = [term(c) for c in range(4)]
    for c in range(4, C):
        sums[c % 4] += term(c)
    return (sums[0] + sums[1]) + (sums[2] + sums[3])


def update_kernel(
    holder, m_ref, g_ref, w_ref, o_hbm, stage, o_ref, o_sem
):
    parts = o_sem.shape[0]
    part = o_ref.shape[1] // parts
    cols = o_ref.shape[2]
    stores = []
    for n in range(parts):
        first = n * part

        def channel(c):
            return m_ref[holder[c], first : first + part, :].astype(F32)

        mean = tree_sum(channel) * (1 / C)
        spread = tree_sum(lambda c: jnp.square(channel(c) - mean)) * (1 / C)
        scale = lax.rsqrt(spread + 1e-05)
        for c in range(C):
            stage[c * PITCH : c * PITCH + part, :] = (channel(c) - mean) * scale
        for s in range(part):
            x = stage[pl.ds(s, C, stride=PITCH), :].astype(BF16)
            p = lax.dot_general(x, w_ref[...], TN, preferred_element_type=F32)
            o_ref[0, first + s] = (p[:cols] * g_ref[0, first + s]).astype(BF16)
            o_ref[1, first + s] = (p[cols:] * g_ref[1, first + s]).astype(BF16)
        at = pl.ds(first, part)
        store = pltpu.make_async_copy(o_ref.at[:, at], o_hbm.at[:, at], o_sem.at[n])
        store.start()
        stores.append(store)
    for store in stores:
        store.wait()


def update(mixed, gate4, w, holder):
    _, steps, cols, ch = gate4.shape
    parts = steps // BLOCK
    hbm = pl.BlockSpec(memory_space=pltpu.HBM)
    sems = pltpu.SemaphoreType.DMA((parts,))
    return pl.pallas_call(
        functools.partial(update_kernel, holder),
        in_specs=[pl.BlockSpec(memory_space=pltpu.VMEM)] * 3,
        out_specs=hbm,
        out_shape=jax.ShapeDtypeStruct(gate4.shape, BF16),
        scratch_shapes=[
            pltpu.VMEM((C * PITCH, 2 * cols), F32),
            pltpu.VMEM(gate4.shape, BF16),
            sems,
        ],
        compiler_params=pltpu.CompilerParams(vmem_limit_bytes=VMEM),
        cost_estimate=pl.CostEstimate(
            flops=2 * C * C * 8192, bytes_accessed=8 << 20, transcendentals=0
        ),
        name="update",
    )(mixed, gate4, w)


FIRST = ("xl", "xh", "y", "core", "z")
SECOND = ("core", "y", "xl", "xh", "z")
SIZES = {"z": 4, "xh": 2, "xl": 2, "y": 4, "core": 2}
AXES = tuple(SIZES)


def places(order):
    counts = np.arange(128).reshape([SIZES[axis] for axis in order])
    return counts.transpose([order.index(axis) for axis in AXES]).reshape(8, 16)


def on_device(pair, left_gate, left_proj, right_gate, right_proj, out_gate, out_proj):
    first, second = places(FIRST), places(SECOND)
    holder = np.empty(128, int)
    holder[first.reshape(-1)] = second.reshape(-1)
    ni, nj, ch = pair.shape
    pair4 = pair.reshape(2, ni // 2, nj, ch)
    sent, gate = edges(pair4, left_gate, left_proj, right_gate, right_proj, out_gate)
    got = lax.all_to_all(sent, FIRST, 0, 0, tiled=True)
    mixed = mix(got, first, second)
    mixed = lax.all_to_all(mixed, SECOND, 0, 0, tiled=True)
    out = update(mixed, gate, out_proj, holder)
    return out.reshape(ni, nj, ch)


def solution(mesh):
    split = jax.sharding.Mesh(mesh.devices.reshape(tuple(SIZES.values())), AXES)
    spec = P(("z", "xh"), ("xl", "y", "core"), None)
    return jax.shard_map(
        on_device,
        mesh=split,
        in_specs=(spec, P(), P(), P(), P(), P(), P()),
        out_specs=spec,
        check_vma=False,
    )
```

```python
import functools

import jax
import jax.numpy as jnp
import numpy as np
from jax import lax
from jax.experimental import pallas as pl
from jax.experimental.pallas import tpu as pltpu
from jax.sharding import PartitionSpec as P

C = 128
F32 = jnp.float32
BF16 = jnp.bfloat16
BLOCK = 16
PITCH = BLOCK + 1
VMEM = 24 * 1024 * 1024
FULL = 63 * 1024 * 1024

NT = (((1,), (1,)), ((), ()))
TN = (((0,), (0,)), ((), ()))


def norm_rows(x):
    x = x.astype(F32)
    center = x - jnp.mean(x, axis=-1, keepdims=True)
    spread = jnp.mean(center * center, axis=-1, keepdims=True)
    return (center * lax.rsqrt(spread + 1e-05)).astype(BF16)


def edges_kernel(
    x_hbm, lg_hbm, lp_hbm, rg_hbm, rp_hbm, og_hbm, o_hbm, g_hbm,
    x_ref, o_ref, g_ref, w_in, w_ref, stage_l, stage_r, x_sem, o_sem, g_sem, w_sem
):
    weights = [
        pltpu.make_async_copy(ref, w_in.at[n], w_sem.at[n])
        for n, ref in enumerate((lg_hbm, lp_hbm, rg_hbm, rp_hbm, og_hbm))
    ]
    parts = x_sem.shape[0]
    part = x_ref.shape[1] // parts
    loads = [
        pltpu.make_async_copy(
            x_hbm.at[:, pl.ds(n * part, part)], x_ref.at[:, pl.ds(n * part, part)], x_sem.at[n]
        )
        for n in range(parts)
    ]
    for copy in weights + loads:
        copy.start()
    for n, copy in enumerate(weights):
        copy.wait()
        if n < 4:
            w_ref[n * C : (n + 1) * C, :] = w_in[n].T * 0.5
        else:
            w_in[n] = w_in[n] * 0.5

    for copy in loads:
        copy.wait()
    stores = []
    for n in range(parts):
        first = n * part
        for s in range(0, part, 2):
            x = jnp.concatenate(
                [x_ref[0, first + s], x_ref[1, first + s]]
                + [x_ref[0, first + s + 1], x_ref[1, first + s + 1]],
                axis=0,
            )
            x = norm_rows(x)
            q = jnp.dot(x, w_in[4], preferred_element_type=F32)
            q = (jnp.tanh(q) * 0.5 + 0.5).astype(BF16).reshape(2, 2, -1, C)
            g_ref[0, first + s], g_ref[1, first + s] = q[0, 0], q[0, 1]
            g_ref[0, first + s + 1], g_ref[1, first + s + 1] = q[1, 0], q[1, 1]
            p = lax.dot_general(w_ref[...], x, NT, preferred_element_type=F32)
            for side, stage in enumerate((stage_l, stage_r)):
                at = 2 * C * side
                half = p[at + C : at + 2 * C]
                edge = jnp.tanh(p[at : at + C]) * half + half
                stage[pl.ds(s, C, stride=PITCH), :] = edge[:, :C]
                stage[pl.ds(s + 1, C, stride=PITCH), :] = edge[:, C:]
        for side, stage in enumerate((stage_l, stage_r)):
            for c in range(C):
                o_ref[c, side, first : first + part, :] = stage[
                    c * PITCH : c * PITCH + part, :
                ].astype(BF16)
        at = pl.ds(first, part)
        for store in (
            pltpu.make_async_copy(o_ref.at[:, :, at], o_hbm.at[:, :, at], o_sem.at[n]),
            pltpu.make_async_copy(g_ref.at[:, at], g_hbm.at[:, at], g_sem.at[n]),
        ):
            store.start()
            stores.append(store)
    for store in stores:
        store.wait()


def edges(pair4, lg, lp, rg, rp, og):
    _, steps, cols, ch = pair4.shape
    parts = steps // BLOCK
    hbm = pl.BlockSpec(memory_space=pltpu.HBM)
    stage = pltpu.VMEM((C * PITCH, 2 * cols), F32)
    return pl.pallas_call(
        edges_kernel,
        in_specs=[hbm] * 6,
        out_specs=[hbm, hbm],
        out_shape=[
            jax.ShapeDtypeStruct((C, 2, steps, 2 * cols), BF16),
            jax.ShapeDtypeStruct(pair4.shape, BF16),
        ],
        scratch_shapes=[
            pltpu.VMEM(pair4.shape, BF16),
            pltpu.VMEM((C, 2, steps, 2 * cols), BF16),
            pltpu.VMEM(pair4.shape, BF16),
            pltpu.VMEM((5, C, C), BF16),
            pltpu.VMEM((4 * C, C), BF16),
            stage,
            stage,
            pltpu.SemaphoreType.DMA((parts,)),
            pltpu.SemaphoreType.DMA((parts,)),
            pltpu.SemaphoreType.DMA((parts,)),
            pltpu.SemaphoreType.DMA((5,)),
        ],
        compiler_params=pltpu.CompilerParams(vmem_limit_bytes=FULL),
        cost_estimate=pl.CostEstimate(
            flops=2 * 5 * C * C * 8192, bytes_accessed=8 << 20, transcendentals=2 << 20
        ),
        name="edges",
    )(pair4, lg, lp, rg, rp, og)


def turn(top, low):
    h = top.shape[1] // 2
    return (
        jnp.concatenate([top[:, :h], low[:, :h]], axis=1),
        jnp.concatenate([top[:, h:], low[:, h:]], axis=1),
    )


def mix_kernel(source, target, got_ref, o_ref, left, right):
    rows, cols = source.shape
    s = got_ref.shape[2]
    for side, dst in enumerate((left, right)):
        for r in range(rows):
            for q in range(0, cols, 2):
                a, b = turn(got_ref[source[r, q], side], got_ref[source[r, q + 1], side])
                dst[2 * r * s : 2 * r * s + s, q * s : q * s + 2 * s] = a
                dst[2 * r * s + s : 2 * r * s + 2 * s, q * s : q * s + 2 * s] = b
    wide = 4
    for n in range(0, cols, wide):
        m = lax.dot_general(
            left[...], right[n * s : (n + wide) * s, :], NT, preferred_element_type=F32
        ).astype(BF16)
        for r in range(rows):
            top = m[2 * r * s : 2 * r * s + s]
            low = m[2 * r * s + s : 2 * r * s + 2 * s]
            for q in range(0, wide, 2):
                at = slice(q * s, q * s + 2 * s)
                a, b = turn(top[:, at], low[:, at])
                o_ref[target[r, n + q]] = a
                o_ref[target[r, n + q + 1]] = b


def mix(got, source, target):
    count, _, steps, lanes = got.shape
    rows, cols = source.shape
    edge = pltpu.VMEM((2 * rows * steps, cols * steps), BF16)
    return pl.pallas_call(
        functools.partial(mix_kernel, source, target),
        in_specs=[pl.BlockSpec(memory_space=pltpu.VMEM)],
        out_specs=pl.BlockSpec(memory_space=pltpu.VMEM),
        out_shape=jax.ShapeDtypeStruct((count, steps, lanes), BF16),
        scratch_shapes=[edge, edge],
        compiler_params=pltpu.CompilerParams(vmem_limit_bytes=VMEM),
        cost_estimate=pl.CostEstimate(
            flops=2 << 30, bytes_accessed=6 << 20, transcendentals=0
        ),
        name="mix",
    )(got)


def tree_sum(term):
    sums = [term(c) for c in range(4)]
    for c in range(4, C):
        sums[c % 4] += term(c)
    return (sums[0] + sums[1]) + (sums[2] + sums[3])


def update_kernel(
    holder, m_ref, g_ref, w_ref, o_hbm, stage, o_ref, o_sem
):
    parts = o_sem.shape[0]
    part = o_ref.shape[1] // parts
    cols = o_ref.shape[2]
    stores = []
    for n in range(parts):
        first = n * part

        def channel(c):
            return m_ref[holder[c], first : first + part, :].astype(F32)

        mean = tree_sum(channel) * (1 / C)
        spread = tree_sum(lambda c: jnp.square(channel(c) - mean)) * (1 / C)
        scale = lax.rsqrt(spread + 1e-05)
        for c in range(C):
            stage[c * PITCH : c * PITCH + part, :] = (channel(c) - mean) * scale
        for s in range(part):
            x = stage[pl.ds(s, C, stride=PITCH), :].astype(BF16)
            p = lax.dot_general(x, w_ref[...], TN, preferred_element_type=F32)
            o_ref[0, first + s] = (p[:cols] * g_ref[0, first + s]).astype(BF16)
            o_ref[1, first + s] = (p[cols:] * g_ref[1, first + s]).astype(BF16)
        at = pl.ds(first, part)
        store = pltpu.make_async_copy(o_ref.at[:, at], o_hbm.at[:, at], o_sem.at[n])
        store.start()
        stores.append(store)
    for store in stores:
        store.wait()


def update(mixed, gate4, w, holder):
    _, steps, cols, ch = gate4.shape
    parts = steps // BLOCK
    hbm = pl.BlockSpec(memory_space=pltpu.HBM)
    sems = pltpu.SemaphoreType.DMA((parts,))
    return pl.pallas_call(
        functools.partial(update_kernel, holder),
        in_specs=[pl.BlockSpec(memory_space=pltpu.VMEM)] * 3,
        out_specs=hbm,
        out_shape=jax.ShapeDtypeStruct(gate4.shape, BF16),
        scratch_shapes=[
            pltpu.VMEM((C * PITCH, 2 * cols), F32),
            pltpu.VMEM(gate4.shape, BF16),
            sems,
        ],
        compiler_params=pltpu.CompilerParams(vmem_limit_bytes=VMEM),
        cost_estimate=pl.CostEstimate(
            flops=2 * C * C * 8192, bytes_accessed=8 << 20, transcendentals=0
        ),
        name="update",
    )(mixed, gate4, w)


FIRST = ("z", "xl", "xh", "core", "y")
SECOND = ("core", "y", "xh", "xl", "z")
SIZES = {"z": 4, "xh": 2, "xl": 2, "y": 4, "core": 2}
AXES = tuple(SIZES)


def places(order):
    counts = np.arange(128).reshape([SIZES[axis] for axis in order])
    return counts.transpose([order.index(axis) for axis in AXES]).reshape(8, 16)


def on_device(pair, left_gate, left_proj, right_gate, right_proj, out_gate, out_proj):
    first, second = places(FIRST), places(SECOND)
    holder = np.empty(128, int)
    holder[first.reshape(-1)] = second.reshape(-1)
    ni, nj, ch = pair.shape
    pair4 = pair.reshape(2, ni // 2, nj, ch)
    sent, gate = edges(pair4, left_gate, left_proj, right_gate, right_proj, out_gate)
    got = lax.all_to_all(sent, FIRST, 0, 0, tiled=True)
    mixed = mix(got, first, second)
    mixed = lax.all_to_all(mixed, SECOND, 0, 0, tiled=True)
    out = update(mixed, gate, out_proj, holder)
    return out.reshape(ni, nj, ch)


def solution(mesh):
    split = jax.sharding.Mesh(mesh.devices.reshape(tuple(SIZES.values())), AXES)
    spec = P(("z", "xh"), ("xl", "y", "core"), None)
    return jax.shard_map(
        on_device,
        mesh=split,
        in_specs=(spec, P(), P(), P(), P(), P(), P()),
        out_specs=spec,
        check_vma=False,
    )
```

```python
import functools

import jax
import jax.numpy as jnp
import numpy as np
from jax import lax
from jax.experimental import pallas as pl
from jax.experimental.pallas import tpu as pltpu
from jax.sharding import PartitionSpec as P

C = 128
F32 = jnp.float32
BF16 = jnp.bfloat16
BLOCK = 16
PITCH = BLOCK + 1
VMEM = 24 * 1024 * 1024
FULL = 63 * 1024 * 1024

NT = (((1,), (1,)), ((), ()))
TN = (((0,), (0,)), ((), ()))


def norm_rows(x):
    x = x.astype(F32)
    center = x - jnp.mean(x, axis=-1, keepdims=True)
    spread = jnp.mean(center * center, axis=-1, keepdims=True)
    return (center * lax.rsqrt(spread + 1e-05)).astype(BF16)


def edges_kernel(
    x_hbm, lg_hbm, lp_hbm, rg_hbm, rp_hbm, og_hbm, o_hbm, g_hbm,
    x_ref, o_ref, g_ref, w_in, w_ref, stage_l, stage_r, x_sem, o_sem, g_sem, w_sem
):
    weights = [
        pltpu.make_async_copy(ref, w_in.at[n], w_sem.at[n])
        for n, ref in enumerate((lg_hbm, lp_hbm, rg_hbm, rp_hbm, og_hbm))
    ]
    parts = x_sem.shape[0]
    part = x_ref.shape[1] // parts
    loads = [
        pltpu.make_async_copy(
            x_hbm.at[:, pl.ds(n * part, part)], x_ref.at[:, pl.ds(n * part, part)], x_sem.at[n]
        )
        for n in range(parts)
    ]
    for copy in weights + loads:
        copy.start()
    for n, copy in enumerate(weights):
        copy.wait()
        if n < 4:
            w_ref[n * C : (n + 1) * C, :] = w_in[n].T * 0.5
        else:
            w_in[n] = w_in[n] * 0.5

    for copy in loads:
        copy.wait()
    stores = []
    for n in range(parts):
        first = n * part
        for s in range(0, part, 2):
            x = jnp.concatenate(
                [x_ref[0, first + s], x_ref[1, first + s]]
                + [x_ref[0, first + s + 1], x_ref[1, first + s + 1]],
                axis=0,
            )
            x = norm_rows(x)
            q = jnp.dot(x, w_in[4], preferred_element_type=F32)
            q = (jnp.tanh(q) * 0.5 + 0.5).astype(BF16).reshape(2, 2, -1, C)
            g_ref[0, first + s], g_ref[1, first + s] = q[0, 0], q[0, 1]
            g_ref[0, first + s + 1], g_ref[1, first + s + 1] = q[1, 0], q[1, 1]
            p = lax.dot_general(w_ref[...], x, NT, preferred_element_type=F32)
            for side, stage in enumerate((stage_l, stage_r)):
                at = 2 * C * side
                half = p[at + C : at + 2 * C]
                edge = jnp.tanh(p[at : at + C]) * half + half
                stage[pl.ds(s, C, stride=PITCH), :] = edge[:, :C]
                stage[pl.ds(s + 1, C, stride=PITCH), :] = edge[:, C:]
        for side, stage in enumerate((stage_l, stage_r)):
            for c in range(C):
                o_ref[c, side, first : first + part, :] = stage[
                    c * PITCH : c * PITCH + part, :
                ].astype(BF16)
        at = pl.ds(first, part)
        for store in (
            pltpu.make_async_copy(o_ref.at[:, :, at], o_hbm.at[:, :, at], o_sem.at[n]),
            pltpu.make_async_copy(g_ref.at[:, at], g_hbm.at[:, at], g_sem.at[n]),
        ):
            store.start()
            stores.append(store)
    for store in stores:
        store.wait()


def edges(pair4, lg, lp, rg, rp, og):
    _, steps, cols, ch = pair4.shape
    parts = steps // BLOCK
    hbm = pl.BlockSpec(memory_space=pltpu.HBM)
    stage = pltpu.VMEM((C * PITCH, 2 * cols), F32)
    return pl.pallas_call(
        edges_kernel,
        in_specs=[hbm] * 6,
        out_specs=[hbm, hbm],
        out_shape=[
            jax.ShapeDtypeStruct((C, 2, steps, 2 * cols), BF16),
            jax.ShapeDtypeStruct(pair4.shape, BF16),
        ],
        scratch_shapes=[
            pltpu.VMEM(pair4.shape, BF16),
            pltpu.VMEM((C, 2, steps, 2 * cols), BF16),
            pltpu.VMEM(pair4.shape, BF16),
            pltpu.VMEM((5, C, C), BF16),
            pltpu.VMEM((4 * C, C), BF16),
            stage,
            stage,
            pltpu.SemaphoreType.DMA((parts,)),
            pltpu.SemaphoreType.DMA((parts,)),
            pltpu.SemaphoreType.DMA((parts,)),
            pltpu.SemaphoreType.DMA((5,)),
        ],
        compiler_params=pltpu.CompilerParams(vmem_limit_bytes=FULL),
        cost_estimate=pl.CostEstimate(
            flops=2 * 5 * C * C * 8192, bytes_accessed=8 << 20, transcendentals=2 << 20
        ),
        name="edges",
    )(pair4, lg, lp, rg, rp, og)


def turn(top, low):
    h = top.shape[1] // 2
    return (
        jnp.concatenate([top[:, :h], low[:, :h]], axis=1),
        jnp.concatenate([top[:, h:], low[:, h:]], axis=1),
    )


def mix_kernel(source, target, got_ref, o_ref, left, right):
    rows, cols = source.shape
    s = got_ref.shape[2]
    for side, dst in enumerate((left, right)):
        for r in range(rows):
            for q in range(0, cols, 2):
                a, b = turn(got_ref[source[r, q], side], got_ref[source[r, q + 1], side])
                dst[2 * r * s : 2 * r * s + s, q * s : q * s + 2 * s] = a
                dst[2 * r * s + s : 2 * r * s + 2 * s, q * s : q * s + 2 * s] = b
    wide = 4
    for n in range(0, cols, wide):
        m = lax.dot_general(
            left[...], right[n * s : (n + wide) * s, :], NT, preferred_element_type=F32
        ).astype(BF16)
        for r in range(rows):
            top = m[2 * r * s : 2 * r * s + s]
            low = m[2 * r * s + s : 2 * r * s + 2 * s]
            for q in range(0, wide, 2):
                at = slice(q * s, q * s + 2 * s)
                a, b = turn(top[:, at], low[:, at])
                o_ref[target[r, n + q]] = a
                o_ref[target[r, n + q + 1]] = b


def mix(got, source, target):
    count, _, steps, lanes = got.shape
    rows, cols = source.shape
    edge = pltpu.VMEM((2 * rows * steps, cols * steps), BF16)
    return pl.pallas_call(
        functools.partial(mix_kernel, source, target),
        in_specs=[pl.BlockSpec(memory_space=pltpu.VMEM)],
        out_specs=pl.BlockSpec(memory_space=pltpu.VMEM),
        out_shape=jax.ShapeDtypeStruct((count, steps, lanes), BF16),
        scratch_shapes=[edge, edge],
        compiler_params=pltpu.CompilerParams(vmem_limit_bytes=VMEM),
        cost_estimate=pl.CostEstimate(
            flops=2 << 30, bytes_accessed=6 << 20, transcendentals=0
        ),
        name="mix",
    )(got)


def tree_sum(term):
    sums = [term(c) for c in range(4)]
    for c in range(4, C):
        sums[c % 4] += term(c)
    return (sums[0] + sums[1]) + (sums[2] + sums[3])


def update_kernel(
    holder, m_ref, g_ref, w_ref, o_hbm, stage, o_ref, o_sem
):
    parts = o_sem.shape[0]
    part = o_ref.shape[1] // parts
    cols = o_ref.shape[2]
    stores = []
    for n in range(parts):
        first = n * part

        def channel(c):
            return m_ref[holder[c], first : first + part, :].astype(F32)

        mean = tree_sum(channel) * (1 / C)
        spread = tree_sum(lambda c: jnp.square(channel(c) - mean)) * (1 / C)
        scale = lax.rsqrt(spread + 1e-05)
        for c in range(C):
            stage[c * PITCH : c * PITCH + part, :] = (channel(c) - mean) * scale
        for s in range(part):
            x = stage[pl.ds(s, C, stride=PITCH), :].astype(BF16)
            p = lax.dot_general(x, w_ref[...], TN, preferred_element_type=F32)
            o_ref[0, first + s] = (p[:cols] * g_ref[0, first + s]).astype(BF16)
            o_ref[1, first + s] = (p[cols:] * g_ref[1, first + s]).astype(BF16)
        at = pl.ds(first, part)
        store = pltpu.make_async_copy(o_ref.at[:, at], o_hbm.at[:, at], o_sem.at[n])
        store.start()
        stores.append(store)
    for store in stores:
        store.wait()


def update(mixed, gate4, w, holder):
    _, steps, cols, ch = gate4.shape
    parts = steps // BLOCK
    hbm = pl.BlockSpec(memory_space=pltpu.HBM)
    sems = pltpu.SemaphoreType.DMA((parts,))
    return pl.pallas_call(
        functools.partial(update_kernel, holder),
        in_specs=[pl.BlockSpec(memory_space=pltpu.VMEM)] * 3,
        out_specs=hbm,
        out_shape=jax.ShapeDtypeStruct(gate4.shape, BF16),
        scratch_shapes=[
            pltpu.VMEM((C * PITCH, 2 * cols), F32),
            pltpu.VMEM(gate4.shape, BF16),
            sems,
        ],
        compiler_params=pltpu.CompilerParams(vmem_limit_bytes=VMEM),
        cost_estimate=pl.CostEstimate(
            flops=2 * C * C * 8192, bytes_accessed=8 << 20, transcendentals=0
        ),
        name="update",
    )(mixed, gate4, w)


FIRST = ("core", "y", "xh", "xl", "z")
SECOND = ("core", "y", "xh", "xl", "z")
SIZES = {"z": 4, "xh": 2, "xl": 2, "y": 4, "core": 2}
AXES = tuple(SIZES)


def places(order):
    counts = np.arange(128).reshape([SIZES[axis] for axis in order])
    return counts.transpose([order.index(axis) for axis in AXES]).reshape(8, 16)


def on_device(pair, left_gate, left_proj, right_gate, right_proj, out_gate, out_proj):
    first, second = places(FIRST), places(SECOND)
    holder = np.empty(128, int)
    holder[first.reshape(-1)] = second.reshape(-1)
    ni, nj, ch = pair.shape
    pair4 = pair.reshape(2, ni // 2, nj, ch)
    sent, gate = edges(pair4, left_gate, left_proj, right_gate, right_proj, out_gate)
    got = lax.all_to_all(sent, FIRST, 0, 0, tiled=True)
    mixed = mix(got, first, second)
    mixed = lax.all_to_all(mixed, SECOND, 0, 0, tiled=True)
    out = update(mixed, gate, out_proj, holder)
    return out.reshape(ni, nj, ch)


def solution(mesh):
    split = jax.sharding.Mesh(mesh.devices.reshape(tuple(SIZES.values())), AXES)
    spec = P(("z", "xh"), ("xl", "y", "core"), None)
    return jax.shard_map(
        on_device,
        mesh=split,
        in_specs=(spec, P(), P(), P(), P(), P(), P()),
        out_specs=spec,
        check_vma=False,
    )
```
